256 devices in a mesh: rcv: 256 (over x, z, y, core).
Axes of the slice: x: 4, y: 4, z: 8, core: 2. Of those that a mesh axis runs over, the one named last changes fastest.
Arguments:
- predictions: bfloat16 [262144, 384], P('rcv'), may hold values from -6 to 6
- observed: bfloat16 [2, 262144, 1024], P(None, 'rcv'), may hold values from -0.3984375 to 0.3984375
- partners: int32 [2, 256], replicated, may hold values from 0 to 255, as said below
- green_block: bfloat16 [262144, 512], P('rcv'), may hold values from -0.046875 to 0.046875
Outputs:
- gradient: float32 [512, 384], P('rcv')
The draws below stay inside these ranges and needn't reach their ends.
Inputs may be any that keep to these rules, and one draw needn't show every extreme that they name: `partners`: row m pairs block b with block b XOR s_m for a meeting offset s_m; s_0 lies in 1 to 254 and s_1 = s_0 XOR (255).
All inputs are finite; a program needn't handle non-finite values.
Results may differ from the reference program's by a relative error of at most 0.0034.
Values may be sent and summed in bfloat16 or wider, within the bound.
A program may use at most 64 MiB of HBM per device.

```python
import jax
import jax.numpy as jnp
from jax import lax

R_DEV = 1024
NT = 384
CELLS = 512
MEET = 2
RT = 262144
N_RCV = 256


def draw_partners(key, part):
    first = jax.random.randint(key, (), 1, N_RCV - 1).astype(jnp.int32)
    second = jnp.bitwise_xor(first, N_RCV - 1)
    blocks = jnp.arange(N_RCV, dtype=jnp.int32)
    return jnp.stack([jnp.bitwise_xor(blocks, first), jnp.bitwise_xor(blocks, second)]).astype(jnp.int32)


def spiked(array, own_key, source, target, shards_of, factor):
    def block_of(position):
        return (jnp.arange(array.shape[position]) // (array.shape[position] // shards_of)).reshape((-1,) + (1,) * (array.ndim - 1 - position))

    one_side = jax.random.permutation(own_key, shards_of)[block_of(target)]
    second = (block_of(target) + shards_of // 2) % shards_of
    return jnp.where((block_of(source) == one_side) | (block_of(source) == second), factor * array, array)


def block_scale(stream_key, extent, pieces, smallest, top_value):
    level = 1.0
    for dim, shards_of in pieces:
        steps = jax.random.uniform(jax.random.fold_in(jax.random.fold_in(stream_key, 6), dim), (shards_of,), jnp.float32, smallest / len(pieces), top_value / len(pieces))
        level = level * jnp.repeat(jnp.exp(steps), extent[dim] // shards_of).reshape((-1,) + (1,) * (len(extent) - 1 - dim))
    return level


def noise(key, shape, scale, bound, pieces=(), kind=jnp.bfloat16):
    level = block_scale(key, shape, pieces, -0.22, 0.18) if pieces else 1.0
    result = jax.random.normal(key, shape, jnp.float32) * scale * level
    return jnp.minimum(jnp.maximum(result, -bound), bound).astype(kind)


def heavy_noise(own_key, extent, spread, limit, split, heavy, kind=jnp.bfloat16):
    array = spread * jax.random.normal(own_key, extent, jnp.float32)
    if split:
        array = array * block_scale(own_key, extent, split, -0.22, 0.18)
    return jnp.clip(spiked(array, jax.random.fold_in(own_key, 3), *heavy), -limit, limit).astype(kind)


def setup_inputs(seed: int = 0) -> dict:
    keys = jax.random.split(jax.random.key(seed), 5)
    return {
        "predictions": noise(keys[0], (RT, NT), 1.0, 6.0, ((0, 256),)),
        "observed": noise(keys[1], (MEET, RT, R_DEV), 0.05, 0.3984375, ((1, 256),)),
        "partners": draw_partners(jax.random.fold_in(keys[4], 71), 0),
        "green_block": heavy_noise(keys[3], (RT, CELLS), RT ** -0.5, 0.046875, ((0, 256),), (0, 1, 256, 6.0)),
    }


student_nu = 0.01


def reference(predictions, observed, partners, green_block):
    inverse = 1.0 / NT
    blocks = predictions.reshape(N_RCV, R_DEV, NT)
    tiles = observed.reshape(MEET, N_RCV, R_DEV, R_DEV)

    def one_block(device):
        mine = lax.dynamic_index_in_dim(blocks, device, 0, keepdims=False)
        own_sum = jnp.zeros((R_DEV, NT), jnp.float32)
        backs = []
        for meeting in range(MEET):
            partner = partners[meeting, device].astype(jnp.int32)
            other = lax.dynamic_index_in_dim(blocks, partner, 0, keepdims=False)
            tile_obs = lax.dynamic_index_in_dim(tiles[meeting], device, 0, keepdims=False)
            gram_tile = lax.dot_general(mine, other, (((1,), (1,)), ((), ())), preferred_element_type=jnp.float32)
            residual = gram_tile * inverse - tile_obs.astype(jnp.float32)
            weights = ((student_nu + 1.0) * residual / (student_nu + residual * residual)).astype(jnp.bfloat16)
            own_sum = own_sum + jnp.dot(weights, other, preferred_element_type=jnp.float32) * inverse
            back_rows = lax.dot_general(weights, mine, (((0,), (0,)), ((), ())), preferred_element_type=jnp.float32) * inverse
            backs.append(back_rows.astype(jnp.bfloat16))
        return own_sum, jnp.stack(backs)

    own_all, back_all = lax.map(one_block, jnp.arange(N_RCV, dtype=jnp.int32))
    adjoint = own_all
    for meeting in range(MEET):
        adjoint = adjoint + jnp.take(back_all[:, meeting], partners[meeting].astype(jnp.int32), axis=0).astype(jnp.float32)
    adjoint = adjoint.astype(jnp.bfloat16).reshape(RT, NT)
    return lax.dot_general(green_block, adjoint, (((0,), (0,)), ((), ())), preferred_element_type=jnp.float32)
```

```python
import functools

import jax
import jax.numpy as jnp
from jax import lax
from jax.experimental import pallas as pl
from jax.experimental.pallas import tpu as pltpu
from jax.sharding import PartitionSpec as P

STUDENT_NU = 0.01
MESH = pl.DeviceIdType.MESH
CHUNK = 128
ROWS = 256
CORE_BITS, Y_BITS, Z_BITS, X_BITS = 1, 2, 3, 2


def flipped(index, mask):
    return lax.bitwise_xor(index, jnp.int32(mask))


def remote(src, dst, send, recv, target):
    return pltpu.make_async_remote_copy(
        src_ref=src, dst_ref=dst, send_sem=send, recv_sem=recv, device_id=(target,), device_id_type=MESH
    )


def greet(peers):
    barrier = pltpu.get_barrier_semaphore()
    for peer in peers:
        pl.semaphore_signal(barrier, inc=1, device_id=(peer,), device_id_type=MESH)
    pl.semaphore_wait(barrier, len(peers))


def cell_order(shape):
    row = lax.broadcasted_iota(jnp.int32, shape, 0)
    pair = row & 1
    z = (row >> 1) & (2**Z_BITS - 1)
    x = (row >> (1 + Z_BITS)) & (2**X_BITS - 1)
    y = (row >> (1 + Z_BITS + X_BITS)) & (2**Y_BITS - 1)
    core = row >> (1 + Z_BITS + X_BITS + Y_BITS)
    device = (((x << Z_BITS) + z << Y_BITS) + y << CORE_BITS) + core
    return device * 2 + pair


def pair_tile(mine, partner_rows, tile_obs):
    inverse = 1.0 / mine.shape[1]
    gram_tile = lax.dot_general(
        mine, partner_rows, (((1,), (1,)), ((), ())), preferred_element_type=jnp.float32
    )
    residual = gram_tile * inverse - tile_obs.astype(jnp.float32)
    weights = ((STUDENT_NU + 1.0) * residual / (STUDENT_NU + residual * residual)).astype(jnp.bfloat16)
    own_part = jnp.dot(weights, partner_rows, preferred_element_type=jnp.float32) * inverse
    back_rows = (
        lax.dot_general(weights, mine, (((0,), (0,)), ((), ())), preferred_element_type=jnp.float32)
        * inverse
    )
    return (own_part, back_rows.astype(jnp.bfloat16))


def sum_kernel(part_ref, out_ref, got_core, held, got_plane, piece, got_line, sc, rc, sp, rp, sl, rl):
    me = lax.axis_index("rcv")
    core = me & 1
    y = (me >> CORE_BITS) & (2**Y_BITS - 1)
    z = (me >> (CORE_BITS + Y_BITS)) & (2**Z_BITS - 1)
    x = me >> (CORE_BITS + Y_BITS + Z_BITS)
    plane = 2 ** (X_BITS + Y_BITS)
    line = 2**Z_BITS
    spot = y * 2**X_BITS + x

    def plane_mask(k):
        kx, ky = k % 2**X_BITS, k // 2**X_BITS
        return (kx << (CORE_BITS + Y_BITS + Z_BITS)) | (ky << CORE_BITS)

    def line_mask(k):
        return k << (CORE_BITS + Y_BITS)

    twin = flipped(me, 1)
    planes = [flipped(me, plane_mask(k)) for k in range(1, plane)]
    lines = [flipped(me, line_mask(k)) for k in range(1, line)]
    greet([twin] + planes + lines)

    across = remote(part_ref.at[1 - core], got_core, sc, rc, twin)
    across.start()
    across.wait_recv()
    held[...] = part_ref[core] + got_core[...]
    copies = []
    for k in range(1, plane):
        copy = remote(
            held.at[flipped(spot, k)], got_plane.at[k - 1], sp.at[k - 1], rp.at[k - 1], planes[k - 1]
        )
        copy.start()
        copies.append(copy)
    total = held[spot]
    for k in range(1, plane):
        copies[k - 1].wait_recv()
        total = total + got_plane[k - 1]
    for k in range(line):
        piece[k] = total[2 * k : 2 * k + 2]
    for k in range(1, line):
        copy = remote(
            piece.at[flipped(z, k)], got_line.at[k - 1], sl.at[k - 1], rl.at[k - 1], lines[k - 1]
        )
        copy.start()
        copies.append(copy)
    result = piece[z]
    for k in range(1, line):
        copies[plane - 2 + k].wait_recv()
        result = result + got_line[k - 1]
    out_ref[...] = result
    across.wait_send()
    for copy in copies:
        copy.wait_send()


def sum_call(part):
    cells, samples = part.shape
    plane = 2 ** (X_BITS + Y_BITS)
    line = 2**Z_BITS
    lot = cells // (2 * plane)
    dma = pltpu.SemaphoreType.DMA
    return pl.pallas_call(
        sum_kernel,
        out_shape=jax.ShapeDtypeStruct((2, samples), jnp.float32),
        in_specs=[pl.BlockSpec(memory_space=pltpu.VMEM)],
        out_specs=pl.BlockSpec(memory_space=pltpu.VMEM),
        scratch_shapes=[
            pltpu.VMEM((plane, lot, samples), jnp.float32),
            pltpu.VMEM((plane, lot, samples), jnp.float32),
            pltpu.VMEM((plane - 1, lot, samples), jnp.float32),
            pltpu.VMEM((line, 2, samples), jnp.float32),
            pltpu.VMEM((line - 1, 2, samples), jnp.float32),
            dma, dma, dma((plane - 1,)), dma((plane - 1,)), dma((line - 1,)), dma((line - 1,)),
        ],
        compiler_params=pltpu.CompilerParams(collective_id=0, has_side_effects=True),
        name="sum_cells",
    )(part.reshape(2, plane, lot, samples))


def swap_with(mask, devices):
    pairs = [(i, i ^ mask) for i in range(devices)]
    return lambda value: lax.ppermute(value, "rcv", pairs)


def shards(predictions, observed, partners, green_block):
    devices = lax.axis_size("rcv")
    full = devices - 1
    top = devices // 2
    offset = partners[0, 0]
    swapped = offset // top
    low = jnp.where(swapped == 1, lax.bitwise_xor(offset, full), offset)
    moves = [swap_with(mask, devices) for mask in range(1, top)]
    mirror = swap_with(full, devices)
    cells = green_block.shape[1]
    order = (cell_order((cells, cells)) == lax.broadcasted_iota(jnp.int32, (cells, cells), 1)).astype(jnp.bfloat16)
    turned = lax.dot_general(
        order, green_block, (((1,), (1,)), ((), ())), preferred_element_type=jnp.float32
    ).astype(jnp.bfloat16)
    near = lax.switch(low - 1, moves, predictions)
    far = mirror(near)
    own_near, back_near = pair_tile(
        predictions, near, lax.dynamic_index_in_dim(observed, swapped, 0, keepdims=False)
    )
    own_far, back_far = pair_tile(
        predictions, far, lax.dynamic_index_in_dim(observed, 1 - swapped, 0, keepdims=False)
    )
    back = mirror(back_far)
    total = (back_near.astype(jnp.float32) + back.astype(jnp.float32)).astype(jnp.bfloat16)
    home = lax.switch(low - 1, moves, total)
    adjoint = (own_near + own_far + home.astype(jnp.float32)).astype(jnp.bfloat16)
    return sum_call(jnp.dot(turned, adjoint, preferred_element_type=jnp.float32))


def solution(mesh):
    placed = (P("rcv", None), P(None, "rcv", None), P(), P("rcv", None))
    return jax.shard_map(
        shards, mesh=mesh, in_specs=placed, out_specs=P("rcv", None), check_vma=False
    )
```

```python
import functools

import jax
import jax.numpy as jnp
import numpy as np
from jax import lax
from jax.experimental import pallas as pl
from jax.experimental.pallas import tpu as pltpu
from jax.sharding import PartitionSpec as P

STUDENT_NU = 0.01
MESH = pl.DeviceIdType.MESH
CHUNK = 128
ROWS = 512
CORE_BITS, Y_BITS, Z_BITS, X_BITS = 1, 2, 3, 2
STATIC = ("core", "x1", "y1", "x3", "y3")
LAGS = (0, 1, 2, 3, 4, 5, 6, 7, 8, 9, 10, 11, 12, 13)


def flipped(index, mask):
    return lax.bitwise_xor(index, jnp.int32(mask))


def remote(src, dst, send, recv, target):
    return pltpu.make_async_remote_copy(
        src_ref=src, dst_ref=dst, send_sem=send, recv_sem=recv, device_id=(target,), device_id_type=MESH
    )


def greet(peers):
    barrier = pltpu.get_barrier_semaphore()
    for peer in peers:
        pl.semaphore_signal(barrier, inc=1, device_id=(peer,), device_id_type=MESH)
    pl.semaphore_wait(barrier, len(peers))


def cell_order(row):
    pair = row & 1
    z = (row >> 1) & (2**Z_BITS - 1)
    x = (row >> (1 + Z_BITS)) & (2**X_BITS - 1)
    y = (row >> (1 + Z_BITS + X_BITS)) & (2**Y_BITS - 1)
    core = row >> (1 + Z_BITS + X_BITS + Y_BITS)
    device = (((x << Z_BITS) + z << Y_BITS) + y << CORE_BITS) + core
    return device * 2 + pair


def tile_kernel(direct, spec, flag_ref, p_ref, o_hbm, g_hbm, order_hbm, grad_ref, o_ref, g_ref, order_ref, gt_ref, weights, theirs, answers, own, *rest):
    levels, full = spec["levels"], spec["full"]
    names, lags = spec["names"], spec["lags"]
    buffers = dict(zip(names, rest[: len(names)]))
    rest = rest[len(names) :]
    o_sem, g_sem, order_sem = rest[:3]
    sends = rest[3::2]
    receives = rest[4::2]
    me = lax.axis_index("rcv")
    rows, samples = p_ref.shape
    count = rows // CHUNK
    inverse = 1.0 / samples
    peers = [flipped(me, mask) for mask in levels]
    if direct:
        peers.append(flipped(me, direct))
    peers.append(flipped(me, full))

    def part(j):
        return pl.ds(pl.multiple_of(j * CHUNK, CHUNK), CHUNK)

    def copy(k, mask, src, dst):
        return lambda j: remote(
            src.at[part(j)], dst.at[part(j)], sends[k].at[j], receives[k].at[j], flipped(me, mask)
        )

    depth = len(levels)
    held = [p_ref] + [buffers[f"kept{k}"] for k in range(depth)]
    if not direct:
        held[depth] = theirs.at[0]
    out_copies = [copy(k, levels[k], held[k], buffers[f"got{k}"]) for k in range(depth)]
    near, far = theirs.at[0], theirs.at[1]
    v_near, v_far = answers.at[0], answers.at[1]
    back, total = buffers["back"], buffers["total"]
    go_near = copy(depth, direct, held[depth], near) if direct else None
    go_far = copy(depth + 1, full, near, far)
    go_back = copy(depth + 2, full, v_far, back)
    home = buffers["home"] if direct else total
    go_home = copy(depth + 3, direct, total, home) if direct else None
    returned = [home] + [buffers[f"sum{k}"] for k in range(depth)]
    home_copies = [
        copy(depth + 4 + k, levels[depth - 1 - k], returned[k], buffers[f"ret{k}"]) for k in range(depth)
    ]

    o_copy = pltpu.make_async_copy(o_hbm, o_ref, o_sem)
    g_copy = pltpu.make_async_copy(g_hbm, g_ref, g_sem)
    order_copy = pltpu.make_async_copy(order_hbm, order_ref, order_sem)
    o_copy.start()
    g_copy.start()
    order_copy.start()
    greet(peers)

    first_copy = out_copies[0] if depth else go_near

    @pl.loop(0, count)
    def _(j):
        first_copy(j).start()

    o_copy.wait()
    g_copy.wait()
    order_copy.wait()

    @pl.loop(0, rows // ROWS)
    def _(j):
        lines = pl.ds(pl.multiple_of(j * ROWS, ROWS), ROWS)
        gt_ref[:, lines] = lax.dot_general(
            order_ref[...], g_ref[lines], (((1,), (1,)), ((), ())), preferred_element_type=jnp.float32
        ).astype(jnp.bfloat16)

    first = flag_ref[0]

    def choose(k, got, kept, j):
        picked = jnp.broadcast_to(flag_ref[1 + k] == 1, (CHUNK, samples))
        return jnp.where(
            picked, got[part(j)].astype(jnp.float32), kept[part(j)].astype(jnp.float32)
        ).astype(jnp.bfloat16)

    def tile(j, side):
        rows_in = theirs[side, part(j)]
        which = first ^ side

        def block(i, acc):
            lines = pl.ds(pl.multiple_of(i * ROWS, ROWS), ROWS)
            mine = p_ref[lines]
            gram = lax.dot_general(mine, rows_in, (((1,), (1,)), ((), ())), preferred_element_type=jnp.float32)
            residual = gram * inverse - o_ref[which, lines, part(j)].astype(jnp.float32)
            weight = ((STUDENT_NU + 1.0) * residual / (STUDENT_NU + residual * residual)).astype(jnp.bfloat16)
            weights[side, lines, part(j)] = weight
            return acc + lax.dot_general(weight, mine, (((0,), (0,)), ((), ())), preferred_element_type=jnp.float32)

        acc = lax.fori_loop(0, rows // ROWS, block, jnp.zeros((CHUNK, samples), jnp.float32))
        answers[side, part(j)] = (acc * inverse).astype(jnp.bfloat16)

    def level_step(k):
        def run(j):
            out_copies[k](j).wait_recv()
            held[k + 1][part(j)] = choose(k, buffers[f"got{k}"], held[k], j)
            after = out_copies[k + 1] if k + 1 < depth else (go_near if direct else go_far)
            after(j).start()

        return run

    def tile_steps(t, lag_near, lag_far):
        @pl.loop(0, 2)
        def _(side):
            j = t - lag_near - side * (lag_far - lag_near)

            @pl.when((j >= 0) & (j < count))
            def _():
                @pl.when(side == 0)
                def _():
                    if direct:
                        go_near(j).wait_recv()
                        go_far(j).start()

                @pl.when(side == 1)
                def _():
                    go_far(j).wait_recv()

                tile(j, side)

                @pl.when(side == 1)
                def _():
                    go_back(j).start()

    def back_step(j):
        go_back(j).wait_recv()
        total[part(j)] = (
            v_near[part(j)].astype(jnp.float32) + back[part(j)].astype(jnp.float32)
        ).astype(jnp.bfloat16)
        if direct:
            go_home(j).start()
        elif depth:
            home_copies[0](j).start()

    def home_step(j):
        go_home(j).wait_recv()
        if depth:
            home_copies[0](j).start()

    def return_step(k):
        def run(j):
            home_copies[k](j).wait_recv()
            returned[k + 1][part(j)] = choose(depth - 1 - k, buffers[f"ret{k}"], returned[k], j)
            if k + 1 < depth:
                home_copies[k + 1](j).start()

        return run

    def own_step(j):
        own[part(j)] = jnp.dot(weights[0, part(j)], theirs[0], preferred_element_type=jnp.float32) + jnp.dot(
            weights[1, part(j)], theirs[1], preferred_element_type=jnp.float32
        )

    steps = [level_step(k) for k in range(depth)] + ["near", "far", back_step]
    steps += [home_step] if direct else [None]
    steps += [return_step(k) for k in range(depth)]
    when = list(lags[: len(steps)])
    own_lag = when[depth + 1] + count
    assert all(a is not None for a in when)

    @pl.loop(0, count + max(max(when), own_lag))
    def _(t):
        for step, lag in zip(steps, when):
            if step == "near":
                tile_steps(t, lag, when[depth + 1])
            elif step not in (None, "far"):

                @pl.when((t >= lag) & (t < lag + count))
                def _(step=step, lag=lag):
                    step(t - lag)

        @pl.when(t >= own_lag)
        def _():
            @pl.when(t < own_lag + count)
            def _():
                own_step(t - own_lag)

    last = returned[depth]
    grad_ref[...] = jnp.zeros_like(grad_ref)

    @pl.loop(0, rows // 256)
    def _(j):
        lines = pl.ds(pl.multiple_of(j * 256, 256), 256)
        adjoint = (own[lines] * inverse + last[lines].astype(jnp.float32)).astype(jnp.bfloat16)
        grad_ref[...] += jnp.dot(gt_ref[:, lines], adjoint, preferred_element_type=jnp.float32)

    started = out_copies + ([go_near] if direct else []) + [go_far, go_back]
    started += ([go_home] if direct else []) + home_copies

    @pl.loop(0, count)
    def _(j):
        for one in started:
            one(j).wait_send()


def tile_call(direct, spec, identity, flags, predictions, observed, green, order):
    rows, samples = predictions.shape
    count = rows // CHUNK
    cells = green.shape[1]
    depth = len(spec["levels"])
    block = pltpu.VMEM((rows, samples), jnp.bfloat16)
    sems = pltpu.SemaphoreType.DMA((count,))
    anywhere = pl.BlockSpec(memory_space=pl.ANY)
    return pl.pallas_call(
        functools.partial(tile_kernel, direct, spec),
        out_shape=jax.ShapeDtypeStruct((cells, samples), jnp.float32),
        in_specs=[
            pl.BlockSpec(memory_space=pltpu.SMEM),
            pl.BlockSpec(memory_space=pltpu.VMEM),
            anywhere, anywhere, anywhere,
        ],
        out_specs=pl.BlockSpec(memory_space=pltpu.VMEM),
        scratch_shapes=[
            pltpu.VMEM(observed.shape, jnp.bfloat16),
            pltpu.VMEM(green.shape, jnp.bfloat16),
            pltpu.VMEM(order.shape, jnp.bfloat16),
            pltpu.VMEM((cells, rows), jnp.bfloat16),
            pltpu.VMEM((2, rows, rows), jnp.bfloat16),
            pltpu.VMEM((2, rows, samples), jnp.bfloat16),
            pltpu.VMEM((2, rows, samples), jnp.bfloat16),
            pltpu.VMEM((rows, samples), jnp.float32),
            *[block] * len(spec["names"]),
            *[pltpu.SemaphoreType.DMA] * 3,
            *[sems] * (2 * (4 + 2 * depth)),
        ],
        compiler_params=pltpu.CompilerParams(
            collective_id=1 + identity, has_side_effects=True, vmem_limit_bytes=44 * 2**20
        ),
        name=f"tiles_{direct}",
    )(flags, predictions, observed, green, order)


def sum_kernel(part_ref, out_ref, got_core, held, got_plane, piece, got_line, sc, rc, sp, rp, sl, rl):
    me = lax.axis_index("rcv")
    core = me & 1
    y = (me >> CORE_BITS) & (2**Y_BITS - 1)
    z = (me >> (CORE_BITS + Y_BITS)) & (2**Z_BITS - 1)
    x = me >> (CORE_BITS + Y_BITS + Z_BITS)
    plane = 2 ** (X_BITS + Y_BITS)
    line = 2**Z_BITS
    spot = y * 2**X_BITS + x

    def plane_mask(k):
        kx, ky = k % 2**X_BITS, k // 2**X_BITS
        return (kx << (CORE_BITS + Y_BITS + Z_BITS)) | (ky << CORE_BITS)

    def line_mask(k):
        return k << (CORE_BITS + Y_BITS)

    twin = flipped(me, 1)
    planes = [flipped(me, plane_mask(k)) for k in range(1, plane)]
    lines = [flipped(me, line_mask(k)) for k in range(1, line)]
    greet([twin] + planes + lines)

    across = remote(part_ref.at[1 - core], got_core, sc, rc, twin)
    across.start()
    across.wait_recv()
    held[...] = part_ref[core] + got_core[...]
    copies = []
    for k in range(1, plane):
        copy = remote(
            held.at[flipped(spot, k)], got_plane.at[k - 1], sp.at[k - 1], rp.at[k - 1], planes[k - 1]
        )
        copy.start()
        copies.append(copy)
    total = held[spot]
    for k in range(1, plane):
        copies[k - 1].wait_recv()
        total = total + got_plane[k - 1]
    for k in range(line):
        piece[k] = total[2 * k : 2 * k + 2]
    for k in range(1, line):
        copy = remote(
            piece.at[flipped(z, k)], got_line.at[k - 1], sl.at[k - 1], rl.at[k - 1], lines[k - 1]
        )
        copy.start()
        copies.append(copy)
    result = piece[z]
    for k in range(1, line):
        copies[plane - 2 + k].wait_recv()
        result = result + got_line[k - 1]
    out_ref[...] = result
    across.wait_send()
    for copy in copies:
        copy.wait_send()


def sum_call(part):
    cells, samples = part.shape
    plane = 2 ** (X_BITS + Y_BITS)
    line = 2**Z_BITS
    lot = cells // (2 * plane)
    dma = pltpu.SemaphoreType.DMA
    return pl.pallas_call(
        sum_kernel,
        out_shape=jax.ShapeDtypeStruct((2, samples), jnp.float32),
        in_specs=[pl.BlockSpec(memory_space=pltpu.VMEM)],
        out_specs=pl.BlockSpec(memory_space=pltpu.VMEM),
        scratch_shapes=[
            pltpu.VMEM((plane, lot, samples), jnp.float32),
            pltpu.VMEM((plane, lot, samples), jnp.float32),
            pltpu.VMEM((plane - 1, lot, samples), jnp.float32),
            pltpu.VMEM((line, 2, samples), jnp.float32),
            pltpu.VMEM((line - 1, 2, samples), jnp.float32),
            dma, dma, dma((plane - 1,)), dma((plane - 1,)), dma((line - 1,)), dma((line - 1,)),
        ],
        compiler_params=pltpu.CompilerParams(collective_id=0, has_side_effects=True),
        name="sum_cells",
    )(part.reshape(2, plane, lot, samples))


def bit(value, place):
    return lax.shift_right_logical(value, jnp.int32(place)) & 1


def layout():
    y, z, x = CORE_BITS, CORE_BITS + Y_BITS, CORE_BITS + Y_BITS + Z_BITS
    return y, z, x


def shards(predictions, observed, partners, green_block):
    devices = lax.axis_size("rcv")
    full = devices - 1
    y, z, x = layout()
    offset = partners[0, 0]
    swapped = bit(offset, x - 1)
    near = jnp.where(swapped == 1, lax.bitwise_xor(offset, full), offset)
    steps = dict(
        core=(bit(near, 0), 1),
        x1=(bit(near, x) ^ bit(near, x + 1), 1 << x),
        y1=(bit(near, y) ^ bit(near, y + 1), 1 << y),
        x3=(bit(near, x + 1), 3 << x),
        y3=(bit(near, y + 1), 3 << y),
    )
    levels = [steps[name][1] for name in STATIC]
    flags = jnp.stack([swapped] + [steps[name][0] for name in STATIC]).astype(jnp.int32)
    fields = [(bit(near, z + k), 1 << (z + k)) for k in range(Z_BITS - 1)]
    fields += [steps[name] for name in steps if name not in STATIC]
    directs = [0]
    which = jnp.int32(0)
    for k, (value, mask) in enumerate(fields):
        directs = directs + [one ^ mask for one in directs]
        which = which + (value << k)
    depth = len(levels)
    names = [f"got{k}" for k in range(depth)] + [f"kept{k}" for k in range(depth)]
    names += ["back", "total", "home"]
    names += [f"ret{k}" for k in range(depth)] + [f"sum{k}" for k in range(depth)]
    spec = dict(levels=levels, full=full, names=names, lags=LAGS)
    cells = green_block.shape[1]
    order = np.zeros((cells, cells), np.float32)
    order[np.arange(cells), cell_order(np.arange(cells))] = 1.0
    calls = [functools.partial(tile_call, direct, spec, k) for k, direct in enumerate(directs)]
    operands = (flags, predictions, observed, green_block, jnp.asarray(order, jnp.bfloat16))
    part = lax.switch(which, calls, *operands) if len(calls) > 1 else calls[0](*operands)
    return sum_call(part)


def solution(mesh):
    placed = (P("rcv", None), P(None, "rcv", None), P(), P("rcv", None))
    return jax.shard_map(
        shards, mesh=mesh, in_specs=placed, out_specs=P("rcv", None), check_vma=False
    )
```

```python
import functools

import jax
import jax.numpy as jnp
import numpy as np
from jax import lax
from jax.experimental import pallas as pl
from jax.experimental.pallas import tpu as pltpu
from jax.sharding import PartitionSpec as P

STUDENT_NU = 0.01
MESH = pl.DeviceIdType.MESH
CHUNK = 128
ROWS = 256
CORE_BITS, Y_BITS, Z_BITS, X_BITS = 1, 2, 3, 2
STATIC = ("core", "x1", "y1")
LAGS = (0, 1, 2, 3, 4, 5, 6, 7, 8, 9)


def flipped(index, mask):
    return lax.bitwise_xor(index, jnp.int32(mask))


def remote(src, dst, send, recv, target):
    return pltpu.make_async_remote_copy(
        src_ref=src, dst_ref=dst, send_sem=send, recv_sem=recv, device_id=(target,), device_id_type=MESH
    )


def greet(peers):
    barrier = pltpu.get_barrier_semaphore()
    for peer in peers:
        pl.semaphore_signal(barrier, inc=1, device_id=(peer,), device_id_type=MESH)
    pl.semaphore_wait(barrier, len(peers))


def cell_order(row):
    pair = row & 1
    z = (row >> 1) & (2**Z_BITS - 1)
    x = (row >> (1 + Z_BITS)) & (2**X_BITS - 1)
    y = (row >> (1 + Z_BITS + X_BITS)) & (2**Y_BITS - 1)
    core = row >> (1 + Z_BITS + X_BITS + Y_BITS)
    device = (((x << Z_BITS) + z << Y_BITS) + y << CORE_BITS) + core
    return device * 2 + pair


def tile_kernel(direct, spec, flag_ref, p_ref, o_hbm, adjoint_ref, o_ref, weights, theirs, answers, own, *rest):
    levels, full = spec["levels"], spec["full"]
    names, lags = spec["names"], spec["lags"]
    buffers = dict(zip(names, rest[: len(names)]))
    rest = rest[len(names) :]
    o_sem = rest[0]
    sends = rest[1::2]
    receives = rest[2::2]
    me = lax.axis_index("rcv")
    rows, samples = p_ref.shape
    count = rows // CHUNK
    inverse = 1.0 / samples
    peers = [flipped(me, mask) for mask in levels]
    if direct:
        peers.append(flipped(me, direct))
    peers.append(flipped(me, full))

    def part(j):
        return pl.ds(pl.multiple_of(j * CHUNK, CHUNK), CHUNK)

    def copy(k, mask, src, dst):
        return lambda j: remote(
            src.at[part(j)], dst.at[part(j)], sends[k].at[j], receives[k].at[j], flipped(me, mask)
        )

    depth = len(levels)
    held = [p_ref] + [buffers[f"kept{k}"] for k in range(depth)]
    if not direct:
        held[depth] = theirs.at[0]
    out_copies = [copy(k, levels[k], held[k], buffers[f"got{k}"]) for k in range(depth)]
    near, far = theirs.at[0], theirs.at[1]
    v_near, v_far = answers.at[0], answers.at[1]
    back, total = buffers["back"], buffers["total"]
    go_near = copy(depth, direct, held[depth], near) if direct else None
    go_far = copy(depth + 1, full, near, far)
    go_back = copy(depth + 2, full, v_far, back)
    home = buffers["home"] if direct else total
    go_home = copy(depth + 3, direct, total, home) if direct else None
    returned = [home] + [buffers[f"sum{k}"] for k in range(depth)]
    home_copies = [
        copy(depth + 4 + k, levels[depth - 1 - k], returned[k], buffers[f"ret{k}"]) for k in range(depth)
    ]

    o_copy = pltpu.make_async_copy(o_hbm, o_ref, o_sem)
    o_copy.start()
    greet(peers)

    first_copy = out_copies[0] if depth else go_near

    @pl.loop(0, count)
    def _(j):
        first_copy(j).start()

    o_copy.wait()
    first = flag_ref[0]

    def choose(k, got, kept, j):
        picked = jnp.broadcast_to(flag_ref[1 + k] == 1, (CHUNK, samples))
        return jnp.where(
            picked, got[part(j)].astype(jnp.float32), kept[part(j)].astype(jnp.float32)
        ).astype(jnp.bfloat16)

    def tile(j, side):
        rows_in = theirs[side, part(j)]
        which = first ^ side

        def block(i, acc):
            lines = pl.ds(pl.multiple_of(i * ROWS, ROWS), ROWS)
            mine = p_ref[lines]
            gram = lax.dot_general(mine, rows_in, (((1,), (1,)), ((), ())), preferred_element_type=jnp.float32)
            residual = gram * inverse - o_ref[which, lines, part(j)].astype(jnp.float32)
            weight = ((STUDENT_NU + 1.0) * residual / (STUDENT_NU + residual * residual)).astype(jnp.bfloat16)
            weights[side, lines, part(j)] = weight
            return acc + lax.dot_general(weight, mine, (((0,), (0,)), ((), ())), preferred_element_type=jnp.float32)

        acc = lax.fori_loop(0, rows // ROWS, block, jnp.zeros((CHUNK, samples), jnp.float32))
        answers[side, part(j)] = (acc * inverse).astype(jnp.bfloat16)

    def level_step(k):
        def run(j):
            out_copies[k](j).wait_recv()
            held[k + 1][part(j)] = choose(k, buffers[f"got{k}"], held[k], j)
            after = out_copies[k + 1] if k + 1 < depth else (go_near if direct else go_far)
            after(j).start()

        return run

    def tile_steps(t, lag_near, lag_far):
        @pl.loop(0, 2)
        def _(side):
            j = t - lag_near - side * (lag_far - lag_near)

            @pl.when((j >= 0) & (j < count))
            def _():
                @pl.when(side == 0)
                def _():
                    if direct:
                        go_near(j).wait_recv()
                        go_far(j).start()

                @pl.when(side == 1)
                def _():
                    go_far(j).wait_recv()

                tile(j, side)

                @pl.when(side == 1)
                def _():
                    go_back(j).start()

    def back_step(j):
        go_back(j).wait_recv()
        total[part(j)] = (
            v_near[part(j)].astype(jnp.float32) + back[part(j)].astype(jnp.float32)
        ).astype(jnp.bfloat16)
        if direct:
            go_home(j).start()
        elif depth:
            home_copies[0](j).start()

    def home_step(j):
        go_home(j).wait_recv()
        if depth:
            home_copies[0](j).start()

    def return_step(k):
        def run(j):
            home_copies[k](j).wait_recv()
            returned[k + 1][part(j)] = choose(depth - 1 - k, buffers[f"ret{k}"], returned[k], j)
            if k + 1 < depth:
                home_copies[k + 1](j).start()

        return run

    def own_step(j):
        own[part(j)] = jnp.dot(weights[0, part(j)], theirs[0], preferred_element_type=jnp.float32) + jnp.dot(
            weights[1, part(j)], theirs[1], preferred_element_type=jnp.float32
        )

    steps = [level_step(k) for k in range(depth)] + ["near", "far", back_step]
    steps += [home_step] if direct else [None]
    steps += [return_step(k) for k in range(depth)]
    when = list(lags[: len(steps)])
    own_lag = when[depth + 1] + count
    assert all(a is not None for a in when)

    @pl.loop(0, count + max(max(when), own_lag))
    def _(t):
        for step, lag in zip(steps, when):
            if step == "near":
                tile_steps(t, lag, when[depth + 1])
            elif step not in (None, "far"):

                @pl.when((t >= lag) & (t < lag + count))
                def _(step=step, lag=lag):
                    step(t - lag)

        @pl.when(t >= own_lag)
        def _():
            @pl.when(t < own_lag + count)
            def _():
                own_step(t - own_lag)

    last = returned[depth]
    adjoint_ref[...] = (own[...] * inverse + last[...].astype(jnp.float32)).astype(jnp.bfloat16)

    started = out_copies + ([go_near] if direct else []) + [go_far, go_back]
    started += ([go_home] if direct else []) + home_copies

    @pl.loop(0, count)
    def _(j):
        for one in started:
            one(j).wait_send()


def tile_call(direct, spec, identity, flags, predictions, observed):
    rows, samples = predictions.shape
    count = rows // CHUNK
    depth = len(spec["levels"])
    block = pltpu.VMEM((rows, samples), jnp.bfloat16)
    sems = pltpu.SemaphoreType.DMA((count,))
    anywhere = pl.BlockSpec(memory_space=pl.ANY)
    return pl.pallas_call(
        functools.partial(tile_kernel, direct, spec),
        out_shape=jax.ShapeDtypeStruct((rows, samples), jnp.bfloat16),
        in_specs=[
            pl.BlockSpec(memory_space=pltpu.SMEM),
            pl.BlockSpec(memory_space=pltpu.VMEM),
            anywhere,
        ],
        out_specs=pl.BlockSpec(memory_space=pltpu.VMEM),
        scratch_shapes=[
            pltpu.VMEM(observed.shape, jnp.bfloat16),
            pltpu.VMEM((2, rows, rows), jnp.bfloat16),
            pltpu.VMEM((2, rows, samples), jnp.bfloat16),
            pltpu.VMEM((2, rows, samples), jnp.bfloat16),
            pltpu.VMEM((rows, samples), jnp.float32),
            *[block] * len(spec["names"]),
            pltpu.SemaphoreType.DMA,
            *[sems] * (2 * (4 + 2 * depth)),
        ],
        compiler_params=pltpu.CompilerParams(
            collective_id=1 + identity, has_side_effects=True, vmem_limit_bytes=44 * 2**20
        ),
        name=f"tiles_{direct}",
    )(flags, predictions, observed)


def sum_kernel(adjoint_ref, g_ref, order_ref, out_ref, gt_ref, part, got_core, held, got_plane, piece, got_line, sc, rc, sp, rp, sl, rl):
    me = lax.axis_index("rcv")
    core = me & 1
    y = (me >> CORE_BITS) & (2**Y_BITS - 1)
    z = (me >> (CORE_BITS + Y_BITS)) & (2**Z_BITS - 1)
    x = me >> (CORE_BITS + Y_BITS + Z_BITS)
    plane = 2 ** (X_BITS + Y_BITS)
    line = 2**Z_BITS
    spot = y * 2**X_BITS + x

    def plane_mask(k):
        kx, ky = k % 2**X_BITS, k // 2**X_BITS
        return (kx << (CORE_BITS + Y_BITS + Z_BITS)) | (ky << CORE_BITS)

    def line_mask(k):
        return k << (CORE_BITS + Y_BITS)

    twin = flipped(me, 1)
    planes = [flipped(me, plane_mask(k)) for k in range(1, plane)]
    lines = [flipped(me, line_mask(k)) for k in range(1, line)]
    peers = [twin] + planes + lines
    barrier = pltpu.get_barrier_semaphore()
    for peer in peers:
        pl.semaphore_signal(barrier, inc=1, device_id=(peer,), device_id_type=MESH)

    half = got_core.shape[0]
    lot = half // plane

    @pl.loop(0, g_ref.shape[0] // ROWS)
    def _(j):
        lines_in = pl.ds(pl.multiple_of(j * ROWS, ROWS), ROWS)
        gt_ref[:, lines_in] = lax.dot_general(
            order_ref[...], g_ref[lines_in], (((1,), (1,)), ((), ())), preferred_element_type=jnp.float32
        ).astype(jnp.bfloat16)

    @pl.loop(0, 2)
    def _(k):
        side = (1 - core) ^ k
        cells = pl.ds(pl.multiple_of(side * half, half), half)
        part[k] = jnp.dot(gt_ref[cells], adjoint_ref[...], preferred_element_type=jnp.float32)

        @pl.when(k == 0)
        def _():
            pl.semaphore_wait(barrier, len(peers))
            remote(part.at[0], got_core, sc, rc, twin).start()

    across = remote(part.at[0], got_core, sc, rc, twin)
    across.wait_recv()
    held[...] = part[1] + got_core[...]

    def lot_of(index):
        return pl.ds(pl.multiple_of(index * lot, lot), lot)

    copies = []
    for k in range(1, plane):
        copy = remote(
            held.at[lot_of(flipped(spot, k))], got_plane.at[k - 1], sp.at[k - 1], rp.at[k - 1], planes[k - 1]
        )
        copy.start()
        copies.append(copy)
    total = held[lot_of(spot)]
    for k in range(1, plane):
        copies[k - 1].wait_recv()
        total = total + got_plane[k - 1]
    for k in range(line):
        piece[k] = total[2 * k : 2 * k + 2]
    for k in range(1, line):
        copy = remote(
            piece.at[flipped(z, k)], got_line.at[k - 1], sl.at[k - 1], rl.at[k - 1], lines[k - 1]
        )
        copy.start()
        copies.append(copy)
    result = piece[z]
    for k in range(1, line):
        copies[plane - 2 + k].wait_recv()
        result = result + got_line[k - 1]
    out_ref[...] = result
    across.wait_send()
    for copy in copies:
        copy.wait_send()


def sum_call(adjoint, green, order):
    rows, samples = adjoint.shape
    cells = green.shape[1]
    plane = 2 ** (X_BITS + Y_BITS)
    line = 2**Z_BITS
    half = cells // 2
    lot = half // plane
    dma = pltpu.SemaphoreType.DMA
    return pl.pallas_call(
        sum_kernel,
        out_shape=jax.ShapeDtypeStruct((2, samples), jnp.float32),
        in_specs=[pl.BlockSpec(memory_space=pltpu.VMEM)] * 3,
        out_specs=pl.BlockSpec(memory_space=pltpu.VMEM),
        scratch_shapes=[
            pltpu.VMEM((cells, rows), jnp.bfloat16),
            pltpu.VMEM((2, half, samples), jnp.float32),
            pltpu.VMEM((half, samples), jnp.float32),
            pltpu.VMEM((half, samples), jnp.float32),
            pltpu.VMEM((plane - 1, lot, samples), jnp.float32),
            pltpu.VMEM((line, 2, samples), jnp.float32),
            pltpu.VMEM((line - 1, 2, samples), jnp.float32),
            dma, dma, dma((plane - 1,)), dma((plane - 1,)), dma((line - 1,)), dma((line - 1,)),
        ],
        compiler_params=pltpu.CompilerParams(
            collective_id=0, has_side_effects=True, vmem_limit_bytes=20 * 2**20
        ),
        name="sum_cells",
    )(adjoint, green, order)


def bit(value, place):
    return lax.shift_right_logical(value, jnp.int32(place)) & 1


def layout():
    y, z, x = CORE_BITS, CORE_BITS + Y_BITS, CORE_BITS + Y_BITS + Z_BITS
    return y, z, x


def shards(predictions, observed, partners, green_block):
    devices = lax.axis_size("rcv")
    full = devices - 1
    y, z, x = layout()
    offset = partners[0, 0]
    swapped = bit(offset, x - 1)
    near = jnp.where(swapped == 1, lax.bitwise_xor(offset, full), offset)
    steps = dict(
        core=(bit(near, 0), 1),
        x1=(bit(near, x) ^ bit(near, x + 1), 1 << x),
        y1=(bit(near, y) ^ bit(near, y + 1), 1 << y),
        x3=(bit(near, x + 1), 3 << x),
        y3=(bit(near, y + 1), 3 << y),
    )
    levels = [steps[name][1] for name in STATIC]
    flags = jnp.stack([swapped] + [steps[name][0] for name in STATIC]).astype(jnp.int32)
    fields = [(bit(near, z + k), 1 << (z + k)) for k in range(Z_BITS - 1)]
    fields += [steps[name] for name in steps if name not in STATIC]
    directs = [0]
    which = jnp.int32(0)
    for k, (value, mask) in enumerate(fields):
        directs = directs + [one ^ mask for one in directs]
        which = which + (value << k)
    depth = len(levels)
    names = [f"got{k}" for k in range(depth)] + [f"kept{k}" for k in range(depth)]
    names += ["back", "total", "home"]
    names += [f"ret{k}" for k in range(depth)] + [f"sum{k}" for k in range(depth)]
    spec = dict(levels=levels, full=full, names=names, lags=LAGS)
    cells = green_block.shape[1]
    order = np.zeros((cells, cells), np.float32)
    order[np.arange(cells), cell_order(np.arange(cells))] = 1.0
    calls = [functools.partial(tile_call, direct, spec, k) for k, direct in enumerate(directs)]
    operands = (flags, predictions, observed)
    adjoint = lax.switch(which, calls, *operands) if len(calls) > 1 else calls[0](*operands)
    return sum_call(adjoint, green_block, jnp.asarray(order, jnp.bfloat16))


def solution(mesh):
    placed = (P("rcv", None), P(None, "rcv", None), P(), P("rcv", None))
    return jax.shard_map(
        shards, mesh=mesh, in_specs=placed, out_specs=P("rcv", None), check_vma=False
    )
```

```python
import functools

import jax
import jax.numpy as jnp
import numpy as np
from jax import lax
from jax.experimental import pallas as pl
from jax.experimental.pallas import tpu as pltpu
from jax.sharding import PartitionSpec as P

STUDENT_NU = 0.01
MESH = pl.DeviceIdType.MESH
CHUNK = 128
TILE = 256
ROWS = 256
CORE_BITS, Y_BITS, Z_BITS, X_BITS = 1, 2, 3, 2
STATIC = ("core", "x1", "y1")
LAGS = (0, 1, 2, 3, 4, 6, 7, 8, 9, 10)


def flipped(index, mask):
    return lax.bitwise_xor(index, jnp.int32(mask))


def remote(src, dst, send, recv, target):
    return pltpu.make_async_remote_copy(
        src_ref=src, dst_ref=dst, send_sem=send, recv_sem=recv, device_id=(target,), device_id_type=MESH
    )


def greet(peers):
    barrier = pltpu.get_barrier_semaphore()
    for peer in peers:
        pl.semaphore_signal(barrier, inc=1, device_id=(peer,), device_id_type=MESH)
    pl.semaphore_wait(barrier, len(peers))


def cell_order(row):
    pair = row & 1
    z = (row >> 1) & (2**Z_BITS - 1)
    x = (row >> (1 + Z_BITS)) & (2**X_BITS - 1)
    y = (row >> (1 + Z_BITS + X_BITS)) & (2**Y_BITS - 1)
    core = row >> (1 + Z_BITS + X_BITS + Y_BITS)
    device = (((x << Z_BITS) + z << Y_BITS) + y << CORE_BITS) + core
    return device * 2 + pair


def tile_kernel(direct, spec, flag_ref, p_ref, o_hbm, adjoint_ref, o_ref, weights, theirs, answers, own, *rest):
    levels, full = spec["levels"], spec["full"]
    names, lags = spec["names"], spec["lags"]
    buffers = dict(zip(names, rest[: len(names)]))
    rest = rest[len(names) :]
    o_sem = rest[0]
    sends = rest[1::2]
    receives = rest[2::2]
    me = lax.axis_index("rcv")
    rows, samples = p_ref.shape
    count = rows // CHUNK
    inverse = 1.0 / samples
    peers = [flipped(me, mask) for mask in levels]
    if direct:
        peers.append(flipped(me, direct))
    peers.append(flipped(me, full))

    def part(j):
        return pl.ds(pl.multiple_of(j * CHUNK, CHUNK), CHUNK)

    def copy(k, mask, src, dst):
        return lambda j: remote(
            src.at[part(j)], dst.at[part(j)], sends[k].at[j], receives[k].at[j], flipped(me, mask)
        )

    depth = len(levels)
    held = [p_ref] + [buffers[f"kept{k}"] for k in range(depth)]
    if not direct:
        held[depth] = theirs.at[0]
    out_copies = [copy(k, levels[k], held[k], buffers[f"got{k}"]) for k in range(depth)]
    near, far = theirs.at[0], theirs.at[1]
    v_near, v_far = answers.at[0], answers.at[1]
    back, total = buffers["back"], buffers["total"]
    go_near = copy(depth, direct, held[depth], near) if direct else None
    go_far = copy(depth + 1, full, near, far)
    go_back = copy(depth + 2, full, v_far, back)
    home = buffers["home"] if direct else total
    go_home = copy(depth + 3, direct, total, home) if direct else None
    returned = [home] + [buffers[f"sum{k}"] for k in range(depth)]
    home_copies = [
        copy(depth + 4 + k, levels[depth - 1 - k], returned[k], buffers[f"ret{k}"]) for k in range(depth)
    ]

    o_copy = pltpu.make_async_copy(o_hbm, o_ref, o_sem)
    o_copy.start()
    greet(peers)

    first_copy = out_copies[0] if depth else go_near

    @pl.loop(0, count)
    def _(j):
        first_copy(j).start()

    o_copy.wait()
    first = flag_ref[0]

    def choose(k, got, kept, j):
        picked = jnp.broadcast_to(flag_ref[1 + k] == 1, (CHUNK, samples))
        return jnp.where(
            picked, got[part(j)].astype(jnp.float32), kept[part(j)].astype(jnp.float32)
        ).astype(jnp.bfloat16)

    def tile(j, side):
        span = pl.ds(pl.multiple_of(j * TILE, TILE), TILE)
        rows_in = theirs[side, span]
        which = first ^ side

        def block(i, acc):
            lines = pl.ds(pl.multiple_of(i * ROWS, ROWS), ROWS)
            mine = p_ref[lines]
            gram = lax.dot_general(mine, rows_in, (((1,), (1,)), ((), ())), preferred_element_type=jnp.float32)
            residual = gram * inverse - o_ref[which, lines, span].astype(jnp.float32)
            weight = ((STUDENT_NU + 1.0) * residual / (STUDENT_NU + residual * residual)).astype(jnp.bfloat16)
            weights[side, lines, span] = weight
            return acc + lax.dot_general(weight, mine, (((0,), (0,)), ((), ())), preferred_element_type=jnp.float32)

        acc = lax.fori_loop(0, rows // ROWS, block, jnp.zeros((TILE, samples), jnp.float32))
        answers[side, span] = (acc * inverse).astype(jnp.bfloat16)

    def level_step(k):
        def run(j):
            out_copies[k](j).wait_recv()
            held[k + 1][part(j)] = choose(k, buffers[f"got{k}"], held[k], j)
            after = out_copies[k + 1] if k + 1 < depth else (go_near if direct else go_far)
            after(j).start()

        return run

    def near_step(j):
        if direct:
            go_near(j).wait_recv()
            go_far(j).start()

    def far_step(j):
        go_far(j).wait_recv()

    per_tile = TILE // CHUNK

    def tile_step(turn):
        side = turn % 2
        tile(turn // 2, side)

        @pl.when(side == 1)
        def _():
            for k in range(per_tile):
                go_back(turn // 2 * per_tile + k).start()

    def back_step(j):
        go_back(j).wait_recv()
        total[part(j)] = (
            v_near[part(j)].astype(jnp.float32) + back[part(j)].astype(jnp.float32)
        ).astype(jnp.bfloat16)
        if direct:
            go_home(j).start()
        elif depth:
            home_copies[0](j).start()

    def home_step(j):
        go_home(j).wait_recv()
        if depth:
            home_copies[0](j).start()

    def return_step(k):
        def run(j):
            home_copies[k](j).wait_recv()
            returned[k + 1][part(j)] = choose(depth - 1 - k, buffers[f"ret{k}"], returned[k], j)
            if k + 1 < depth:
                home_copies[k + 1](j).start()

        return run

    def own_step(j):
        lines = pl.ds(pl.multiple_of(j * ROWS, ROWS), ROWS)
        own[lines] = jnp.dot(weights[0, lines], theirs[0], preferred_element_type=jnp.float32) + jnp.dot(
            weights[1, lines], theirs[1], preferred_element_type=jnp.float32
        )

    steps = [level_step(k) for k in range(depth)] + [near_step, far_step, back_step]
    steps += [home_step] if direct else [None]
    steps += [return_step(k) for k in range(depth)]
    when = list(lags[: len(steps)])
    tile_lag = when[depth] + TILE // CHUNK - 1
    own_lag = tile_lag + 2 * (rows // TILE)
    assert all(a is not None for a in when)

    @pl.loop(0, max(count + max(when), own_lag + rows // ROWS))
    def _(t):
        for step, lag in zip(steps, when):
            if step is not None:

                @pl.when((t >= lag) & (t < lag + count))
                def _(step=step, lag=lag):
                    step(t - lag)

        @pl.when((t >= tile_lag) & (t < tile_lag + 2 * (rows // TILE)))
        def _():
            tile_step(t - tile_lag)

        @pl.when((t >= own_lag) & (t < own_lag + rows // ROWS))
        def _():
            own_step(t - own_lag)

    last = returned[depth]
    adjoint_ref[...] = (own[...] * inverse + last[...].astype(jnp.float32)).astype(jnp.bfloat16)

    started = out_copies + ([go_near] if direct else []) + [go_far, go_back]
    started += ([go_home] if direct else []) + home_copies

    @pl.loop(0, count)
    def _(j):
        for one in started:
            one(j).wait_send()


def tile_call(direct, spec, identity, flags, predictions, observed):
    rows, samples = predictions.shape
    count = rows // CHUNK
    depth = len(spec["levels"])
    block = pltpu.VMEM((rows, samples), jnp.bfloat16)
    sems = pltpu.SemaphoreType.DMA((count,))
    anywhere = pl.BlockSpec(memory_space=pl.ANY)
    return pl.pallas_call(
        functools.partial(tile_kernel, direct, spec),
        out_shape=jax.ShapeDtypeStruct((rows, samples), jnp.bfloat16),
        in_specs=[
            pl.BlockSpec(memory_space=pltpu.SMEM),
            pl.BlockSpec(memory_space=pltpu.VMEM),
            anywhere,
        ],
        out_specs=pl.BlockSpec(memory_space=pltpu.VMEM),
        scratch_shapes=[
            pltpu.VMEM(observed.shape, jnp.bfloat16),
            pltpu.VMEM((2, rows, rows), jnp.bfloat16),
            pltpu.VMEM((2, rows, samples), jnp.bfloat16),
            pltpu.VMEM((2, rows, samples), jnp.bfloat16),
            pltpu.VMEM((rows, samples), jnp.float32),
            *[block] * len(spec["names"]),
            pltpu.SemaphoreType.DMA,
            *[sems] * (2 * (4 + 2 * depth)),
        ],
        compiler_params=pltpu.CompilerParams(
            collective_id=1 + identity, has_side_effects=True, vmem_limit_bytes=44 * 2**20
        ),
        name=f"tiles_{direct}",
    )(flags, predictions, observed)


def sum_kernel(adjoint_ref, g_ref, order_ref, out_ref, gt_ref, part, got_core, held, got_plane, piece, got_line, sc, rc, sp, rp, sl, rl):
    me = lax.axis_index("rcv")
    core = me & 1
    y = (me >> CORE_BITS) & (2**Y_BITS - 1)
    z = (me >> (CORE_BITS + Y_BITS)) & (2**Z_BITS - 1)
    x = me >> (CORE_BITS + Y_BITS + Z_BITS)
    plane = 2 ** (X_BITS + Y_BITS)
    line = 2**Z_BITS
    spot = y * 2**X_BITS + x

    def plane_mask(k):
        kx, ky = k % 2**X_BITS, k // 2**X_BITS
        return (kx << (CORE_BITS + Y_BITS + Z_BITS)) | (ky << CORE_BITS)

    def line_mask(k):
        return k << (CORE_BITS + Y_BITS)

    twin = flipped(me, 1)
    planes = [flipped(me, plane_mask(k)) for k in range(1, plane)]
    lines = [flipped(me, line_mask(k)) for k in range(1, line)]
    peers = [twin] + planes + lines
    barrier = pltpu.get_barrier_semaphore()
    for peer in peers:
        pl.semaphore_signal(barrier, inc=1, device_id=(peer,), device_id_type=MESH)

    half = got_core.shape[0]
    lot = half // plane

    @pl.loop(0, g_ref.shape[0] // ROWS)
    def _(j):
        lines_in = pl.ds(pl.multiple_of(j * ROWS, ROWS), ROWS)
        gt_ref[:, lines_in] = lax.dot_general(
            order_ref[...], g_ref[lines_in], (((1,), (1,)), ((), ())), preferred_element_type=jnp.float32
        ).astype(jnp.bfloat16)

    @pl.loop(0, 2)
    def _(k):
        side = (1 - core) ^ k
        cells = pl.ds(pl.multiple_of(side * half, half), half)
        part[k] = jnp.dot(gt_ref[cells], adjoint_ref[...], preferred_element_type=jnp.float32)

        @pl.when(k == 0)
        def _():
            pl.semaphore_wait(barrier, len(peers))
            remote(part.at[0], got_core, sc, rc, twin).start()

    across = remote(part.at[0], got_core, sc, rc, twin)
    across.wait_recv()
    held[...] = part[1] + got_core[...]

    def lot_of(index):
        return pl.ds(pl.multiple_of(index * lot, lot), lot)

    copies = []
    for k in range(1, plane):
        copy = remote(
            held.at[lot_of(flipped(spot, k))], got_plane.at[k - 1], sp.at[k - 1], rp.at[k - 1], planes[k - 1]
        )
        copy.start()
        copies.append(copy)
    total = held[lot_of(spot)]
    for k in range(1, plane):
        copies[k - 1].wait_recv()
        total = total + got_plane[k - 1]
    for k in range(line):
        piece[k] = total[2 * k : 2 * k + 2]
    for k in range(1, line):
        copy = remote(
            piece.at[flipped(z, k)], got_line.at[k - 1], sl.at[k - 1], rl.at[k - 1], lines[k - 1]
        )
        copy.start()
        copies.append(copy)
    result = piece[z]
    for k in range(1, line):
        copies[plane - 2 + k].wait_recv()
        result = result + got_line[k - 1]
    out_ref[...] = result
    across.wait_send()
    for copy in copies:
        copy.wait_send()


def sum_call(adjoint, green, order):
    rows, samples = adjoint.shape
    cells = green.shape[1]
    plane = 2 ** (X_BITS + Y_BITS)
    line = 2**Z_BITS
    half = cells // 2
    lot = half // plane
    dma = pltpu.SemaphoreType.DMA
    return pl.pallas_call(
        sum_kernel,
        out_shape=jax.ShapeDtypeStruct((2, samples), jnp.float32),
        in_specs=[pl.BlockSpec(memory_space=pltpu.VMEM)] * 3,
        out_specs=pl.BlockSpec(memory_space=pltpu.VMEM),
        scratch_shapes=[
            pltpu.VMEM((cells, rows), jnp.bfloat16),
            pltpu.VMEM((2, half, samples), jnp.float32),
            pltpu.VMEM((half, samples), jnp.float32),
            pltpu.VMEM((half, samples), jnp.float32),
            pltpu.VMEM((plane - 1, lot, samples), jnp.float32),
            pltpu.VMEM((line, 2, samples), jnp.float32),
            pltpu.VMEM((line - 1, 2, samples), jnp.float32),
            dma, dma, dma((plane - 1,)), dma((plane - 1,)), dma((line - 1,)), dma((line - 1,)),
        ],
        compiler_params=pltpu.CompilerParams(
            collective_id=0, has_side_effects=True, vmem_limit_bytes=20 * 2**20
        ),
        name="sum_cells",
    )(adjoint, green, order)


def bit(value, place):
    return lax.shift_right_logical(value, jnp.int32(place)) & 1


def layout():
    y, z, x = CORE_BITS, CORE_BITS + Y_BITS, CORE_BITS + Y_BITS + Z_BITS
    return y, z, x


def shards(predictions, observed, partners, green_block):
    devices = lax.axis_size("rcv")
    full = devices - 1
    y, z, x = layout()
    offset = partners[0, 0]
    swapped = bit(offset, x - 1)
    near = jnp.where(swapped == 1, lax.bitwise_xor(offset, full), offset)
    steps = dict(
        core=(bit(near, 0), 1),
        x1=(bit(near, x) ^ bit(near, x + 1), 1 << x),
        y1=(bit(near, y) ^ bit(near, y + 1), 1 << y),
        x3=(bit(near, x + 1), 3 << x),
        y3=(bit(near, y + 1), 3 << y),
    )
    levels = [steps[name][1] for name in STATIC]
    flags = jnp.stack([swapped] + [steps[name][0] for name in STATIC]).astype(jnp.int32)
    fields = [(bit(near, z + k), 1 << (z + k)) for k in range(Z_BITS - 1)]
    fields += [steps[name] for name in steps if name not in STATIC]
    directs = [0]
    which = jnp.int32(0)
    for k, (value, mask) in enumerate(fields):
        directs = directs + [one ^ mask for one in directs]
        which = which + (value << k)
    depth = len(levels)
    names = [f"got{k}" for k in range(depth)] + [f"kept{k}" for k in range(depth)]
    names += ["back", "total", "home"]
    names += [f"ret{k}" for k in range(depth)] + [f"sum{k}" for k in range(depth)]
    spec = dict(levels=levels, full=full, names=names, lags=LAGS)
    cells = green_block.shape[1]
    order = np.zeros((cells, cells), np.float32)
    order[np.arange(cells), cell_order(np.arange(cells))] = 1.0
    calls = [functools.partial(tile_call, direct, spec, k) for k, direct in enumerate(directs)]
    operands = (flags, predictions, observed)
    adjoint = lax.switch(which, calls, *operands) if len(calls) > 1 else calls[0](*operands)
    return sum_call(adjoint, green_block, jnp.asarray(order, jnp.bfloat16))


def solution(mesh):
    placed = (P("rcv", None), P(None, "rcv", None), P(), P("rcv", None))
    return jax.shard_map(
        shards, mesh=mesh, in_specs=placed, out_specs=P("rcv", None), check_vma=False
    )
```
